32 devices in a mesh: shard: 8 (over z, x), tensor: 4 (over y, core).
Axes of the slice: x: 2, y: 2, z: 4, core: 2. Of those that a mesh axis runs over, the one named last changes fastest.
Arguments:
- gradient: bfloat16 [768, 3072], P('shard', 'tensor'), may hold values from -0.47851562 to 0.47851562
- moment: float32 [768, 3072], P('shard', 'tensor'), may hold values from -0.48 to 0.48
- second_moment: float32 [768, 3072], P('shard', 'tensor'), may hold values from 0.0001 to 0.01
- stat_left: float32 [768, 768], P('shard', 'tensor'), as said below
- stat_right: float32 [3072, 3072], P('shard', 'tensor'), as said below
- basis_left: float32 [768, 768], P('shard', 'tensor'), as said below
- basis_right: float32 [3072, 3072], P('shard', 'tensor'), as said below
Outputs:
- update: float32 [768, 3072], P('shard', 'tensor')
- moment_new: float32 [768, 3072], P('shard', 'tensor')
- second_new: float32 [768, 3072], P('shard', 'tensor')
- stat_left_new: float32 [768, 768], P('shard', 'tensor')
- stat_right_new: float32 [3072, 3072], P('shard', 'tensor')
- basis_left_new: float32 [768, 768], P('shard', 'tensor')
- basis_right_new: float32 [3072, 3072], P('shard', 'tensor')
The draws below stay inside these ranges and needn't reach their ends.
Inputs may be any that keep to these rules, and one draw needn't show every extreme that they name: `stat_left`: a symmetric matrix. `stat_right`: a symmetric matrix. `basis_left`: a square matrix of full rank. `basis_right`: a square matrix of full rank.
All inputs are finite; a program needn't handle non-finite values.
Results may differ from the reference program's by a relative error of at most 0.0018.
The reference program's roundings to bfloat16 on the way count: a program that leaves them out, or rounds other values in their place, can miss the bound.
Values may be sent and summed in bfloat16 or wider, within the bound.
A program may use at most 64 MiB of HBM per device.

```python
import math
import jax
import jax.numpy as jnp

D = 768
FF = 3072
NS_ITERS = 2


def noise_matrix(key, order):
    return jax.random.normal(key, (order, order), jnp.float32)


def symmetric_stat(key, order, peak):
    key_rank, key_noise = jax.random.split(key)
    ranking = jax.random.permutation(key_rank, order).astype(jnp.float32) + 1.0
    level = peak * jnp.power(ranking, -0.75)
    noise_draw = noise_matrix(key_noise, order)
    off_diagonal = (noise_draw + noise_draw.T) * (0.4 / math.sqrt(2.0 * order))
    scaling = jnp.sqrt(level)
    return scaling[:, None] * scaling[None, :] * (jnp.eye(order, dtype=jnp.float32) + off_diagonal)


def near_identity(key, order):
    noise_draw = noise_matrix(key, order)
    return jnp.eye(order, dtype=jnp.float32) + noise_draw * (0.5 / math.sqrt(order))


def draw_stat_left(key, part):
    return symmetric_stat(jax.random.fold_in(key, 11), D, 40.0)


def draw_stat_right(key, part):
    return symmetric_stat(jax.random.fold_in(key, 23), FF, 10.0)


def draw_basis_left(key, part):
    return near_identity(jax.random.fold_in(key, 37), D)


def draw_basis_right(key, part):
    return near_identity(jax.random.fold_in(key, 41), FF)


def levels(stream_key, shape, cuts, low, high):
    level, own = 1.0, jax.random.fold_in(stream_key, 6)
    for position, parts in cuts:
        heights = jnp.exp(jax.random.uniform(jax.random.fold_in(own, position), (parts,), jnp.float32, low / len(cuts), high / len(cuts)))
        level = level * jnp.repeat(heights, shape[position] // parts).reshape([-1 if axis == position else 1 for axis in range(len(shape))])
    return level


def bell_draw(key, shape, scale, limit, cuts=(), held_as=jnp.bfloat16):
    loudness = levels(key, shape, cuts, -0.22, 0.18) if cuts else 1.0
    entries = jax.random.normal(key, shape, jnp.float32) * scale * loudness
    return jnp.minimum(jnp.maximum(entries, -limit), limit).astype(held_as)


def setup_inputs(seed: int = 0) -> dict:
    key_list = jax.random.split(jax.random.key(seed), 8)
    return {
        "gradient": bell_draw(key_list[0], (D, FF), 0.08, 0.47851562, ((0, 8), (1, 4))),
        "moment": bell_draw(key_list[1], (D, FF), 0.08, 0.48, ((0, 8), (1, 4)), jnp.float32),
        "second_moment": jnp.clip(jnp.exp(math.log(0.01) - 4.6051702 * jax.random.uniform(key_list[2], (D, FF), jnp.float32) ** levels(key_list[2], (D, FF), ((0, 8), (1, 4)), -0.2, 0.2)), 0.0001, 0.01),
        "stat_left": draw_stat_left(jax.random.fold_in(key_list[7], 71), 0),
        "stat_right": draw_stat_right(jax.random.fold_in(key_list[7], 71), 0),
        "basis_left": draw_basis_left(jax.random.fold_in(key_list[7], 71), 0),
        "basis_right": draw_basis_right(jax.random.fold_in(key_list[7], 71), 0),
    }


def orthogonalize(statistic, basis):
    power = jnp.dot(statistic.astype(jnp.bfloat16), basis.astype(jnp.bfloat16), preferred_element_type=jnp.float32)
    iterate = power / jnp.sqrt(jnp.sum(power * power) + 1e-06)
    for iteration in range(NS_ITERS):
        iterate_half = iterate.astype(jnp.bfloat16)
        gram_half = jnp.dot(iterate_half, iterate_half.T, preferred_element_type=jnp.float32).astype(jnp.bfloat16)
        iterate = 1.5 * iterate - 0.5 * jnp.dot(gram_half, iterate_half, preferred_element_type=jnp.float32)
    return iterate

def reference(gradient, moment, second_moment, stat_left, stat_right, basis_left, basis_right):
    stat_left_new = 0.95 * stat_left + 0.05 * jnp.dot(gradient, gradient.T, preferred_element_type=jnp.float32)
    stat_right_new = 0.95 * stat_right + 0.05 * jnp.dot(gradient.T, gradient, preferred_element_type=jnp.float32)
    basis_left_new = orthogonalize(stat_left_new, basis_left)
    basis_right_new = orthogonalize(stat_right_new, basis_right)
    moment_new = 0.9 * moment + 0.1 * gradient.astype(jnp.float32)
    moment_half = moment_new.astype(jnp.bfloat16)
    left_half = basis_left.astype(jnp.bfloat16)
    right_half = basis_right.astype(jnp.bfloat16)
    grad_right = jnp.dot(gradient, right_half, preferred_element_type=jnp.float32).astype(jnp.bfloat16)
    moment_right = jnp.dot(moment_half, right_half, preferred_element_type=jnp.float32).astype(jnp.bfloat16)
    grad_turned = jnp.dot(left_half.T, grad_right, preferred_element_type=jnp.float32)
    moment_turned = jnp.dot(left_half.T, moment_right, preferred_element_type=jnp.float32)
    second_new = 0.95 * second_moment + 0.05 * grad_turned * grad_turned
    scaled = (moment_turned / (jnp.sqrt(second_new) + 1e-08)).astype(jnp.bfloat16)
    back_half = jnp.dot(scaled, right_half.T, preferred_element_type=jnp.float32).astype(jnp.bfloat16)
    update = jnp.dot(left_half, back_half, preferred_element_type=jnp.float32)
    return (update, moment_new, second_new, stat_left_new, stat_right_new, basis_left_new, basis_right_new)
```

```python
import jax
import jax.numpy as jnp
from jax import lax
from jax.sharding import PartitionSpec as P

NS_ITERS = 2
BF16 = jnp.bfloat16
F32 = jnp.float32


def dot(a, b, ca, cb):
    return lax.dot_general(a, b, (((ca,), (cb,)), ((), ())), preferred_element_type=F32)


def pick(array, index, axis):
    return lax.dynamic_index_in_dim(array, index, axis, keepdims=False)


def part(array, index, size, axis):
    return lax.dynamic_slice_in_dim(array, index * size, size, axis)


def gather_blocks(block, n_shard, n_tensor):
    rows, cols = block.shape
    blocks = lax.all_gather(block, ("shard", "tensor"), axis=0, tiled=False)
    blocks = blocks.reshape(n_shard, n_tensor, rows, cols).transpose(0, 2, 1, 3)
    return blocks.reshape(n_shard * rows, n_tensor * cols)


def swap(array, bit, n_tensor):
    return lax.ppermute(array, "tensor", [(i, i ^ bit) for i in range(n_tensor)])


def gram_halves(parts, core, n_tensor, scale):
    half = parts.shape[1] // 2
    mine = part(parts, core, half, 1)
    other = part(parts, 1 - core, half, 1)
    mine = mine + swap(other.astype(BF16), 1, n_tensor).astype(F32)
    bit = 2
    while bit < n_tensor:
        mine = mine + swap(mine.astype(BF16), bit, n_tensor).astype(F32)
        bit *= 2
    if scale is not None:
        mine = (mine * scale) * scale
    mine = mine.astype(BF16)
    return mine, swap(mine, 1, n_tensor)


def apply_gram(halves, panel, core):
    mine, other = halves
    half = mine.shape[1]
    return dot(mine, part(panel, core, half, 0), 1, 0) + dot(
        other, part(panel, 1 - core, half, 0), 1, 0
    )


def make(n_shard, n_tensor):
    def per_device(gradient, moment, second_moment, stat_left, stat_right, basis_left, basis_right):
        s = lax.axis_index("shard")
        t = lax.axis_index("tensor")
        core = t % 2
        rows_left, block_hidden = gradient.shape
        rows_right = stat_right.shape[0]
        block_left = stat_left.shape[1]

        right_columns = lax.all_gather(basis_right.astype(BF16), "shard", axis=0, tiled=True)
        moment_new = 0.9 * moment + 0.1 * gradient.astype(F32)
        both = jnp.stack([gradient, moment_new.astype(BF16)])
        panel = lax.all_gather(gradient, "shard", axis=0, tiled=True)
        both_rows = lax.all_gather(both, "tensor", axis=2, tiled=True)
        left = gather_blocks(basis_left.astype(BF16), n_shard, n_tensor)

        first = s * rows_right
        owner = first // block_hidden
        strip = lax.dynamic_slice_in_dim(panel, first - owner * block_hidden, rows_right, 1)
        strip = lax.psum(jnp.where(t == owner, strip, jnp.zeros_like(strip)), "tensor")
        stat_right_new = 0.95 * stat_right + 0.05 * dot(strip, panel, 0, 0)
        stat_right_rows = lax.all_gather(stat_right_new.astype(BF16), "tensor", axis=1, tiled=True)

        cross_left = lax.psum_scatter(
            dot(gradient, panel, 1, 1), "tensor", scatter_dimension=1, tiled=True
        )
        stat_left_new = 0.95 * stat_left + 0.05 * cross_left
        stat_left_all = gather_blocks(stat_left_new.astype(BF16), n_shard, n_tensor)

        power = dot(stat_right_rows, right_columns, 1, 0)
        square = jnp.sum(lax.all_gather(jnp.sum(power * power), ("shard", "tensor")))
        scale = 1.0 / jnp.sqrt(square + 1e-06)
        power_panel = lax.all_gather(power.astype(BF16), "shard", axis=0, tiled=True)
        parts = dot(power.astype(BF16), power_panel, 1, 1)
        halves = gram_halves(parts, core, n_tensor, scale)
        iterate = scale * (1.5 * power - 0.5 * apply_gram(halves, power_panel, core))
        for _ in range(NS_ITERS - 1):
            iterate_half = iterate.astype(BF16)
            iterate_panel = lax.all_gather(iterate_half, "shard", axis=0, tiled=True)
            halves = gram_halves(dot(iterate_half, iterate_panel, 1, 1), core, n_tensor, None)
            iterate = 1.5 * iterate - 0.5 * apply_gram(halves, iterate_panel, core)

        power_left = dot(stat_left_all, left, 1, 0)
        iterate_left = power_left / jnp.sqrt(jnp.sum(power_left * power_left) + 1e-06)
        for step in range(NS_ITERS):
            left_half = iterate_left.astype(BF16)
            if step < NS_ITERS - 1:
                gram = dot(left_half, left_half, 1, 1).astype(BF16)
                iterate_left = 1.5 * iterate_left - 0.5 * dot(gram, left_half, 1, 0)
            else:
                gram = dot(part(left_half, s, rows_left, 0), left_half, 1, 1).astype(BF16)
                own = part(part(iterate_left, s, rows_left, 0), t, block_left, 1)
                iterate_left = 1.5 * own - 0.5 * dot(gram, part(left_half, t, block_left, 1), 1, 0)

        rotated = lax.dot_general(
            both_rows, right_columns, (((2,), (0,)), ((), ())), preferred_element_type=F32
        ).astype(BF16)
        rotated = lax.all_gather(rotated, "shard", axis=1, tiled=True)
        basis_strip = part(left, s, rows_left, 1)
        grad_turned = dot(basis_strip, rotated[0], 0, 0)
        moment_turned = dot(basis_strip, rotated[1], 0, 0)
        second_new = 0.95 * second_moment + 0.05 * grad_turned * grad_turned
        scaled = (moment_turned / (jnp.sqrt(second_new) + 1e-08)).astype(BF16)
        terms = dot(scaled, right_columns, 1, 1).reshape(rows_left, n_tensor // 2, 2, block_hidden)
        mine = pick(terms, core, 2) + swap(pick(terms, 1 - core, 2), 1, n_tensor)
        pair = t // 2
        count = n_tensor // 2
        while count > 1:
            count //= 2
            mine = mine.reshape(rows_left, 2, count, block_hidden)
            bit = (pair // count) % 2
            mine = pick(mine, bit, 1) + swap(pick(mine, 1 - bit, 1), 2 * count, n_tensor)
        back_half = mine.reshape(rows_left, block_hidden).astype(BF16)
        back_panel = lax.all_gather(back_half, "shard", axis=0, tiled=True)
        update = dot(part(left, s, rows_left, 0), back_panel, 1, 0)
        return (
            update,
            moment_new,
            second_new,
            stat_left_new,
            stat_right_new,
            iterate_left,
            iterate,
        )

    return per_device


def solution(mesh):
    spec = P("shard", "tensor")
    return jax.shard_map(
        make(mesh.shape["shard"], mesh.shape["tensor"]),
        mesh=mesh,
        in_specs=(spec,) * 7,
        out_specs=(spec,) * 7,
        check_vma=False,
    )
```

```python
import functools

import jax
import jax.numpy as jnp
from jax import lax
from jax.experimental import pallas as pl
from jax.experimental.pallas import tpu as pltpu
from jax.sharding import PartitionSpec as P

NS_ITERS = 2
BF16 = jnp.bfloat16
F32 = jnp.float32


def dot(a, b, ca, cb):
    return lax.dot_general(a, b, (((ca,), (cb,)), ((), ())), preferred_element_type=F32)


def pick(array, index, axis):
    return lax.dynamic_index_in_dim(array, index, axis, keepdims=False)


def part(array, index, size, axis):
    return lax.dynamic_slice_in_dim(array, index * size, size, axis)


def gather_kernel(n_chain, n_tensor, n_across, n_along, *refs):
    count = n_across + n_along
    ins, outs = refs[:count], refs[count : 2 * count]
    local_sem = refs[2 * count]
    sems = refs[2 * count + 1 :]
    s, t = lax.axis_index("shard"), lax.axis_index("tensor")
    a, b = s // 2, s % 2
    pair = (a * 2 + 1 - b, t)
    right = (lax.rem(a + 1, n_chain) * 2 + b, t)
    left = (lax.rem(a + n_chain - 1, n_chain) * 2 + b, t)
    near_t = t + 1 - 2 * (t % 2)
    far_t = lax.rem(t + n_tensor // 2, n_tensor)
    near, far = (s, near_t), (s, far_t)
    others = ([pair, right, left] if n_across else []) + ([near, far] if n_along else [])
    barrier = pltpu.get_barrier_semaphore()
    for other in others:
        pl.semaphore_signal(barrier, inc=1, device_id=other, device_id_type=pl.DeviceIdType.MESH)
    pl.semaphore_wait(barrier, len(others))

    def copy(i, block, send, target, own=False):
        send_sem, recv_sem = sems[2 * i], sems[2 * i + 1]
        return pltpu.make_async_remote_copy(
            src_ref=ins[i] if own else outs[i].at[block],
            dst_ref=outs[i].at[block],
            send_sem=send_sem.at[send],
            recv_sem=recv_sem.at[block],
            device_id=target,
            device_id_type=pl.DeviceIdType.MESH,
        )

    has_right, has_left = a + 1 < n_chain, a >= 1
    for i in range(n_across):
        pl.when(has_right)(lambda i=i: copy(i, s, a, right, True).start())
        pl.when(has_left)(lambda i=i: copy(i, s, 2 * n_chain, left, True).start())
        copy(i, s, n_chain + a, pair, True).start()
    for i in range(n_across, count):
        copy(i, t, 0, far, True).start()
        copy(i, t, 1, near, True).start()
    locals_ = []
    for i in range(count):
        own = pltpu.make_async_copy(ins[i], outs[i].at[s if i < n_across else t], local_sem.at[i])
        own.start()
        locals_.append(own)
    if n_across:

        def step(k, carry):
            for i in range(n_across):

                @pl.when(a - k >= 0)
                def _():
                    block = (a - k) * 2 + b
                    copy(i, block, a - k, right).wait_recv()
                    pl.when(has_right)(lambda: copy(i, block, a - k, right).start())
                    copy(i, block, n_chain + a - k, pair).start()

                @pl.when(a + k < n_chain)
                def _():
                    block = (a + k) * 2 + b
                    copy(i, block, a + k, left).wait_recv()
                    pl.when(has_left)(lambda: copy(i, block, a + k, left).start())
                    copy(i, block, n_chain + a + k, pair).start()

            return carry

        lax.fori_loop(1, n_chain, step, 0)
    for i in range(n_across, count):
        copy(i, far_t, 2, near).wait_recv()
        copy(i, far_t, 2, near).start()
    if n_across:

        def finish(j, carry):
            for i in range(n_across):
                block = j * 2 + 1 - b
                copy(i, block, n_chain + j, pair).wait_recv()
                copy(i, j * 2 + b, n_chain + j, pair).wait_send()
                pl.when((j <= a) & has_right)(lambda: copy(i, j * 2 + b, j, right).wait_send())
                pl.when((j > a) & has_left)(lambda: copy(i, j * 2 + b, j, left).wait_send())
            return carry

        lax.fori_loop(0, n_chain, finish, 0)
        for i in range(n_across):
            pl.when(has_left)(lambda i=i: copy(i, s, 2 * n_chain, left).wait_send())
    near_far = near_t + far_t - t
    for i in range(n_across, count):
        copy(i, near_t, 1, near).wait_recv()
        copy(i, near_far, 2, near).wait_recv()
        for send in range(3):
            copy(i, t, send, near).wait_send()
    for own in locals_:
        own.wait()


def gather(name, across, along, n_shard, n_tensor):
    arrays = list(across) + list(along)
    counts = [n_shard] * len(across) + [n_tensor] * len(along)
    scratch = [pltpu.SemaphoreType.DMA((len(arrays),))]
    for n in counts:
        sends = n + 1 if n == n_shard else 3
        scratch += [pltpu.SemaphoreType.DMA((sends,)), pltpu.SemaphoreType.DMA((n,))]
    return pl.pallas_call(
        functools.partial(gather_kernel, n_shard // 2, n_tensor, len(across), len(along)),
        out_shape=[jax.ShapeDtypeStruct((n, *x.shape), x.dtype) for n, x in zip(counts, arrays)],
        in_specs=[pl.BlockSpec(memory_space=pl.ANY)] * len(arrays),
        out_specs=[pl.BlockSpec(memory_space=pl.ANY)] * len(arrays),
        scratch_shapes=scratch,
        compiler_params=pltpu.CompilerParams(collective_id=name, has_side_effects=True),
        name="gather",
    )(*arrays)


def side_by_side(blocks):
    n, rows, cols = blocks.shape
    return blocks.transpose(1, 0, 2).reshape(rows, n * cols)


def stacked(blocks):
    return blocks.reshape(-1, blocks.shape[-1])


def lanes(array):
    return array.reshape(-1, 128)


def swap(array, bit, n_tensor):
    return lax.ppermute(array, "tensor", [(i, i ^ bit) for i in range(n_tensor)])


def gram_halves(parts, core, n_tensor, scale):
    half = parts.shape[1] // 2
    mine = part(parts, core, half, 1)
    other = part(parts, 1 - core, half, 1)
    mine = mine + swap(other.astype(BF16), 1, n_tensor).astype(F32)
    bit = 2
    while bit < n_tensor:
        mine = mine + swap(mine.astype(BF16), bit, n_tensor).astype(F32)
        bit *= 2
    if scale is not None:
        mine = (mine * scale) * scale
    mine = mine.astype(BF16)
    return mine, swap(mine, 1, n_tensor)


def apply_gram(halves, panel, core):
    mine, other = halves
    half = mine.shape[1]
    return dot(mine, part(panel, core, half, 0), 1, 0) + dot(
        other, part(panel, 1 - core, half, 0), 1, 0
    )


def scatter_sum(terms, t, n_tensor):
    rows = terms.shape[0]
    width = terms.shape[1] // n_tensor
    terms = terms.reshape(rows, n_tensor // 2, 2, width)
    core = t % 2
    mine = pick(terms, core, 2) + swap(pick(terms, 1 - core, 2), 1, n_tensor)
    pair = t // 2
    count = n_tensor // 2
    while count > 1:
        count //= 2
        mine = mine.reshape(rows, 2, count, width)
        bit = (pair // count) % 2
        mine = pick(mine, bit, 1) + swap(pick(mine, 1 - bit, 1), 2 * count, n_tensor)
    return mine.reshape(rows, width)


def whole_sum(value, n_tensor):
    bit = 1
    while bit < n_tensor:
        value = value + swap(value, bit, n_tensor)
        bit *= 2
    return value


def make(n_shard, n_tensor):
    def per_device(gradient, moment, second_moment, stat_left, stat_right, basis_left, basis_right):
        s = lax.axis_index("shard")
        t = lax.axis_index("tensor")
        core = t % 2
        rows_left, block_hidden = gradient.shape
        rows_right = stat_right.shape[0]
        block_left = stat_left.shape[1]
        run = functools.partial(gather, n_shard=n_shard, n_tensor=n_tensor)

        moment_new = 0.9 * moment + 0.1 * gradient.astype(F32)
        panel, left_blocks, right_columns, grad_rows, moment_rows = run(
            0,
            [gradient, lanes(basis_left.astype(BF16)), basis_right.astype(BF16)],
            [gradient, moment_new.astype(BF16)],
        )
        panel, right_columns = stacked(panel), stacked(right_columns)
        first = s * rows_right
        owner = first // block_hidden
        strip = lax.dynamic_slice_in_dim(panel, first - owner * block_hidden, rows_right, 1)
        strips, left = run(1, [], [strip, lanes(left_blocks.reshape(-1, block_left))])
        left = side_by_side(left.reshape(n_tensor, n_shard * rows_left, block_left))
        strip = pick(strips, owner, 0)
        stat_right_new = 0.95 * stat_right + 0.05 * dot(strip, panel, 0, 0)
        cross_left = scatter_sum(dot(gradient, panel, 1, 1), t, n_tensor)
        stat_left_new = 0.95 * stat_left + 0.05 * cross_left
        stat_right_rows, stat_left_rows = run(
            2, [], [stat_right_new.astype(BF16), lanes(stat_left_new.astype(BF16))]
        )

        power = dot(side_by_side(stat_right_rows), right_columns, 1, 0)
        power_half = power.astype(BF16)
        square = jnp.full((8, 128), jnp.sum(power * power), F32)
        grad_right = dot(side_by_side(grad_rows), right_columns, 1, 0).astype(BF16)
        moment_right = dot(side_by_side(moment_rows), right_columns, 1, 0).astype(BF16)
        power_panel, squares, stat_left_all, grad_right, moment_right = run(
            3, [power_half, square, lanes(stat_left_rows.reshape(-1, 128)), grad_right, moment_right], []
        )
        power_panel = stacked(power_panel)

        square = whole_sum(jnp.sum(squares[:, 0, 0]), n_tensor)
        scale = 1.0 / jnp.sqrt(square + 1e-06)
        halves = gram_halves(dot(power_half, power_panel, 1, 1), core, n_tensor, scale)
        iterate = scale * (1.5 * power - 0.5 * apply_gram(halves, power_panel, core))

        basis_strip = part(left, s, rows_left, 1)
        grad_turned = dot(basis_strip, stacked(grad_right), 0, 0)
        moment_turned = dot(basis_strip, stacked(moment_right), 0, 0)
        second_new = 0.95 * second_moment + 0.05 * grad_turned * grad_turned
        scaled = (moment_turned / (jnp.sqrt(second_new) + 1e-08)).astype(BF16)
        back_half = scatter_sum(dot(scaled, right_columns, 1, 1), t, n_tensor).astype(BF16)

        update = None
        for step in range(NS_ITERS - 1):
            iterate_half = iterate.astype(BF16)
            sent = [iterate_half] + ([back_half] if step == 0 else [])
            gathered = run(4 + step, sent, [])
            iterate_panel = stacked(gathered[0])
            if step == 0:
                update = dot(part(left, s, rows_left, 0), stacked(gathered[1]), 1, 0)
            halves = gram_halves(dot(iterate_half, iterate_panel, 1, 1), core, n_tensor, None)
            iterate = 1.5 * iterate - 0.5 * apply_gram(halves, iterate_panel, core)

        stat_left_all = stat_left_all.reshape(n_shard, n_tensor, rows_left, block_left)
        stat_left_all = stat_left_all.transpose(0, 2, 1, 3).reshape(left.shape)
        power_left = dot(stat_left_all, left, 1, 0)
        iterate_left = power_left / jnp.sqrt(jnp.sum(power_left * power_left) + 1e-06)
        for step in range(NS_ITERS):
            left_half = iterate_left.astype(BF16)
            if step < NS_ITERS - 1:
                gram = dot(left_half, left_half, 1, 1).astype(BF16)
                iterate_left = 1.5 * iterate_left - 0.5 * dot(gram, left_half, 1, 0)
            else:
                gram = dot(part(left_half, s, rows_left, 0), left_half, 1, 1).astype(BF16)
                own = part(part(iterate_left, s, rows_left, 0), t, block_left, 1)
                iterate_left = 1.5 * own - 0.5 * dot(gram, part(left_half, t, block_left, 1), 1, 0)

        return (
            update,
            moment_new,
            second_new,
            stat_left_new,
            stat_right_new,
            iterate_left,
            iterate,
        )

    return per_device


def solution(mesh):
    spec = P("shard", "tensor")
    return jax.shard_map(
        make(mesh.shape["shard"], mesh.shape["tensor"]),
        mesh=mesh,
        in_specs=(spec,) * 7,
        out_specs=(spec,) * 7,
        check_vma=False,
    )
```

```python
import functools

import jax
import jax.numpy as jnp
from jax import lax
from jax.experimental import pallas as pl
from jax.experimental.pallas import tpu as pltpu
from jax.sharding import PartitionSpec as P

NS_ITERS = 2
BF16 = jnp.bfloat16
F32 = jnp.float32


def dot(a, b, ca, cb):
    return lax.dot_general(a, b, (((ca,), (cb,)), ((), ())), preferred_element_type=F32)


def pick(array, index, axis):
    return lax.dynamic_index_in_dim(array, index, axis, keepdims=False)


def part(array, index, size, axis):
    return lax.dynamic_slice_in_dim(array, index * size, size, axis)


def later_rows(rows, n_chain):
    return rows // (2 * (n_chain - 1)) // 16 * 16


def gather_kernel(n_chain, n_tensor, n_across, n_along, n_swap, pieces, *refs):
    count = n_across + n_along + n_swap
    ins, outs = refs[:count], refs[count : 2 * count]
    local_sem = refs[2 * count]
    sems = refs[2 * count + 1 :]
    s, t = lax.axis_index("shard"), lax.axis_index("tensor")
    a, b = s // 2, s % 2
    pair = (a * 2 + 1 - b, t)
    right = (lax.rem(a + 1, n_chain) * 2 + b, t)
    left = (lax.rem(a + n_chain - 1, n_chain) * 2 + b, t)
    near_t = t + 1 - 2 * (t % 2)
    far_t = lax.rem(t + n_tensor // 2, n_tensor)
    near, far = (s, near_t), (s, far_t)
    others = ([pair, right, left] if n_across else []) + ([near] if n_along else [])
    others += [far] if n_along or n_swap else []
    barrier = pltpu.get_barrier_semaphore()
    for other in others:
        pl.semaphore_signal(barrier, inc=1, device_id=other, device_id_type=pl.DeviceIdType.MESH)
    pl.semaphore_wait(barrier, len(others))

    def remote(src, dst, send_sem, recv_sem, target):
        return pltpu.make_async_remote_copy(
            src_ref=src,
            dst_ref=dst,
            send_sem=send_sem,
            recv_sem=recv_sem,
            device_id=target,
            device_id_type=pl.DeviceIdType.MESH,
        )

    def across(p, block, send, target, own=False):
        i, first, rows, _ = pieces[p]
        dst = outs[i].at[block, pl.ds(first, rows)]
        src = ins[i].at[pl.ds(first, rows)] if own else dst
        return remote(src, dst, sems[2 * p].at[send], sems[2 * p + 1].at[block], target)

    def along(i, block, send, target, own=False):
        pos = 2 * (len(pieces) + i - n_across)
        dst = outs[i].at[block]
        src = ins[i] if own else dst
        return remote(src, dst, sems[pos].at[send], sems[pos + 1].at[block], target)

    def swap(i):
        pos = 2 * (len(pieces) + i - n_across)
        return remote(ins[i], outs[i], sems[pos].at[0], sems[pos + 1].at[0], far)

    has_right, has_left = a + 1 < n_chain, a >= 1
    extra = 2 * n_chain
    order = sorted(range(len(pieces)), key=lambda p: not pieces[p][3])
    for p in order:
        pl.when(has_right)(lambda p=p: across(p, s, a, right, True).start())
        pl.when(has_left)(lambda p=p: across(p, s, extra, left, True).start())
        across(p, s, extra + 2 if pieces[p][3] else n_chain + a, pair, True).start()
    for i in range(n_across, n_across + n_along):
        along(i, t, 0, far, True).start()
        along(i, t, 1, near, True).start()
    for i in range(n_across + n_along, count):
        swap(i).start()
    locals_ = []
    for i in range(n_across + n_along):
        own = pltpu.make_async_copy(ins[i], outs[i].at[s if i < n_across else t], local_sem.at[i])
        own.start()
        locals_.append(own)
    for p in order:
        if pieces[p][3]:
            block = a * 2 + 1 - b
            across(p, block, extra + 2, pair).wait_recv()
            pl.when(has_right)(lambda p=p, block=block: across(p, block, n_chain + a, right).start())
            pl.when(has_left)(lambda p=p, block=block: across(p, block, extra + 1, left).start())

    def step(k, carry):
        for p in order:
            pair_first = pieces[p][3]
            for side in range(2 if pair_first else 1):
                col = 1 - b if side else b

                @pl.when(a - k >= 0)
                def _():
                    block = (a - k) * 2 + col
                    send = side * n_chain + a - k
                    across(p, block, send, right).wait_recv()
                    pl.when(has_right)(lambda: across(p, block, send, right).start())
                    if not pair_first:
                        across(p, block, n_chain + a - k, pair).start()

                @pl.when(a + k < n_chain)
                def _():
                    block = (a + k) * 2 + col
                    send = side * n_chain + a + k
                    across(p, block, send, left).wait_recv()
                    pl.when(has_left)(lambda: across(p, block, send, left).start())
                    if not pair_first:
                        across(p, block, n_chain + a + k, pair).start()

        return carry

    if n_across:
        lax.fori_loop(1, n_chain - 1, step, 0)
    for i in range(n_across, n_across + n_along):
        along(i, far_t, 2, near).wait_recv()
        along(i, far_t, 2, near).start()
    if n_across:
        step(n_chain - 1, 0)

        def finish(j, carry):
            for p in order:
                pair_first = pieces[p][3]
                if not pair_first:
                    across(p, j * 2 + 1 - b, n_chain + j, pair).wait_recv()
                    across(p, j * 2 + b, n_chain + j, pair).wait_send()
                for side in range(2 if pair_first else 1):
                    block = j * 2 + (1 - b if side else b)
                    send = side * n_chain + j
                    pl.when((j <= a) & has_right)(lambda: across(p, block, send, right).wait_send())
                    pl.when((j > a) & has_left)(lambda: across(p, block, send, left).wait_send())
            return carry

        lax.fori_loop(0, n_chain, finish, 0)
        for p in order:
            pl.when(has_left)(lambda p=p: across(p, s, extra, left).wait_send())
            if pieces[p][3]:
                pl.when(has_left)(lambda p=p: across(p, s, extra + 1, left).wait_send())
                across(p, s, extra + 2, pair).wait_send()
    near_far = near_t + far_t - t
    for i in range(n_across, n_across + n_along):
        along(i, near_t, 1, near).wait_recv()
        along(i, near_far, 2, near).wait_recv()
        for send in range(3):
            along(i, t, send, near).wait_send()
    for i in range(n_across + n_along, count):
        swap(i).wait()
    for own in locals_:
        own.wait()


def gather(name, across, along, swaps=(), *, n_shard, n_tensor):
    arrays = list(across) + list(along) + list(swaps)
    pieces = []
    for i, x in enumerate(across):
        later = later_rows(x.shape[0], n_shard // 2)
        pieces.append((i, 0, x.shape[0] - later, False))
        if later:
            pieces.append((i, x.shape[0] - later, later, True))
    shapes = [(n_shard, *x.shape) for x in across]
    shapes += [(n_tensor, *x.shape) for x in along] + [x.shape for x in swaps]
    counts = [(n_shard + 3, n_shard)] * len(pieces) + [(3, n_tensor)] * len(along) + [(1, 1)] * len(swaps)
    scratch = [pltpu.SemaphoreType.DMA((len(arrays),))]
    for sends, receives in counts:
        scratch += [pltpu.SemaphoreType.DMA((sends,)), pltpu.SemaphoreType.DMA((receives,))]
    return pl.pallas_call(
        functools.partial(
            gather_kernel, n_shard // 2, n_tensor, len(across), len(along), len(swaps), tuple(pieces)
        ),
        out_shape=[jax.ShapeDtypeStruct(shape, x.dtype) for shape, x in zip(shapes, arrays)],
        in_specs=[pl.BlockSpec(memory_space=pl.ANY)] * len(arrays),
        out_specs=[pl.BlockSpec(memory_space=pl.ANY)] * len(arrays),
        scratch_shapes=scratch,
        compiler_params=pltpu.CompilerParams(collective_id=name, has_side_effects=True),
        name="gather",
    )(*arrays)


def side_by_side(blocks):
    n, rows, cols = blocks.shape
    return blocks.transpose(1, 0, 2).reshape(rows, n * cols)


def stacked(blocks):
    return blocks.reshape(-1, blocks.shape[-1])


def lanes(array):
    return array.reshape(-1, 128)


def swap(array, bit, n_tensor):
    return lax.ppermute(array, "tensor", [(i, i ^ bit) for i in range(n_tensor)])


def gram_half(parts, core, n_tensor):
    half = parts.shape[1] // 2
    mine = part(parts, core, half, 1)
    other = part(parts, 1 - core, half, 1)
    return mine + swap(other.astype(BF16), 1, n_tensor).astype(F32)


def apply_gram(halves, panel, core):
    mine, other = halves
    half = mine.shape[1]
    return dot(mine, part(panel, core, half, 0), 1, 0) + dot(
        other, part(panel, 1 - core, half, 0), 1, 0
    )


def scatter_sum(terms, t, n_tensor):
    rows = terms.shape[0]
    width = terms.shape[1] // n_tensor
    terms = terms.reshape(rows, n_tensor // 2, 2, width)
    core = t % 2
    mine = pick(terms, core, 2) + swap(pick(terms, 1 - core, 2), 1, n_tensor)
    pair = t // 2
    count = n_tensor // 2
    while count > 1:
        count //= 2
        mine = mine.reshape(rows, 2, count, width)
        bit = (pair // count) % 2
        mine = pick(mine, bit, 1) + swap(pick(mine, 1 - bit, 1), 2 * count, n_tensor)
    return mine.reshape(rows, width)


def whole_sum(value, n_tensor):
    bit = 1
    while bit < n_tensor:
        value = value + swap(value, bit, n_tensor)
        bit *= 2
    return value


def make(n_shard, n_tensor):
    def per_device(gradient, moment, second_moment, stat_left, stat_right, basis_left, basis_right):
        s = lax.axis_index("shard")
        t = lax.axis_index("tensor")
        core = t % 2
        rows_left, block_hidden = gradient.shape
        rows_right = stat_right.shape[0]
        block_left = stat_left.shape[1]
        run = functools.partial(gather, n_shard=n_shard, n_tensor=n_tensor)

        moment_new = 0.9 * moment + 0.1 * gradient.astype(F32)
        third = rows_right // 3
        thirds = [part(basis_right, k, third, 0).astype(BF16) for k in range(3)]
        panel, left_blocks, right_0, grad_rows, moment_rows = run(
            0,
            [gradient, lanes(basis_left.astype(BF16)), thirds[0]],
            [gradient, moment_new.astype(BF16)],
        )
        panel = stacked(panel)
        first = s * rows_right
        owner = first // block_hidden
        strip = lax.dynamic_slice_in_dim(panel, first - owner * block_hidden, rows_right, 1)
        right_1, strips, left = run(1, [thirds[1]], [strip, lanes(left_blocks.reshape(-1, block_left))])
        left = side_by_side(left.reshape(n_tensor, n_shard * rows_left, block_left))
        strip = pick(strips, owner, 0)
        stat_right_new = 0.95 * stat_right + 0.05 * dot(strip, panel, 0, 0)
        cross_left = scatter_sum(dot(gradient, panel, 1, 1), t, n_tensor)
        stat_left_new = 0.95 * stat_left + 0.05 * cross_left
        right_2, stat_left_columns, stat_right_rows = run(
            2, [thirds[2], lanes(stat_left_new.astype(BF16))], [stat_right_new.astype(BF16)]
        )
        right_columns = stacked(jnp.concatenate([right_0, right_1, right_2], axis=1))

        power = dot(side_by_side(stat_right_rows), right_columns, 1, 0)
        power_half = power.astype(BF16)
        square = jnp.full((8, 128), jnp.sum(power * power), F32)
        grad_right = dot(side_by_side(grad_rows), right_columns, 1, 0).astype(BF16)
        moment_right = dot(side_by_side(moment_rows), right_columns, 1, 0).astype(BF16)
        power_panel, squares = run(3, [power_half, square], [])
        power_panel = stacked(power_panel)

        square = whole_sum(jnp.sum(squares[:, 0, 0]), n_tensor)
        scale = 1.0 / jnp.sqrt(square + 1e-06)
        mine = gram_half(dot(power_half, power_panel, 1, 1), core, n_tensor)
        grad_right, moment_right, stat_left_all, there = run(
            4, [grad_right, moment_right], [lanes(stat_left_columns.reshape(-1, 128))], [mine.astype(BF16)]
        )
        mine = (((mine + there.astype(F32)) * scale) * scale).astype(BF16)
        halves = mine, swap(mine, 1, n_tensor)
        iterate = scale * (1.5 * power - 0.5 * apply_gram(halves, power_panel, core))

        basis_strip = part(left, s, rows_left, 1)
        grad_turned = dot(basis_strip, stacked(grad_right), 0, 0)
        moment_turned = dot(basis_strip, stacked(moment_right), 0, 0)
        second_new = 0.95 * second_moment + 0.05 * grad_turned * grad_turned
        scaled = (moment_turned / (jnp.sqrt(second_new) + 1e-08)).astype(BF16)
        back_half = scatter_sum(dot(scaled, right_columns, 1, 1), t, n_tensor).astype(BF16)

        def left_basis():
            stat_all = side_by_side(stat_left_all.reshape(n_tensor, n_shard * rows_left, block_left))
            power_left = dot(stat_all, left, 1, 0)
            iterate_left = power_left / jnp.sqrt(jnp.sum(power_left * power_left) + 1e-06)
            for step in range(NS_ITERS):
                left_half = iterate_left.astype(BF16)
                if step < NS_ITERS - 1:
                    gram = dot(left_half, left_half, 1, 1).astype(BF16)
                    iterate_left = 1.5 * iterate_left - 0.5 * dot(gram, left_half, 1, 0)
                else:
                    gram = dot(part(left_half, s, rows_left, 0), left_half, 1, 1).astype(BF16)
                    own = part(part(iterate_left, s, rows_left, 0), t, block_left, 1)
                    iterate_left = 1.5 * own - 0.5 * dot(gram, part(left_half, t, block_left, 1), 1, 0)
            return iterate_left

        update = None
        for step in range(NS_ITERS - 1):
            iterate_half = iterate.astype(BF16)
            sent = [iterate_half] + ([back_half] if step == 0 else [])
            gathered = run(5 + step, sent, [])
            iterate_panel = stacked(gathered[0])
            if step == 0:
                update = dot(part(left, s, rows_left, 0), stacked(gathered[1]), 1, 0)
            mine = gram_half(dot(iterate_half, iterate_panel, 1, 1), core, n_tensor)
            there = swap(mine.astype(BF16), n_tensor // 2, n_tensor)
            if step == NS_ITERS - 2:
                there, iterate_left, update = lax.optimization_barrier((there, left_basis(), update))
            mine = (mine + there.astype(F32)).astype(BF16)
            halves = mine, swap(mine, 1, n_tensor)
            iterate = 1.5 * iterate - 0.5 * apply_gram(halves, iterate_panel, core)

        return (
            update,
            moment_new,
            second_new,
            stat_left_new,
            stat_right_new,
            iterate_left,
            iterate,
        )

    return per_device


def solution(mesh):
    spec = P("shard", "tensor")
    return jax.shard_map(
        make(mesh.shape["shard"], mesh.shape["tensor"]),
        mesh=mesh,
        in_specs=(spec,) * 7,
        out_specs=(spec,) * 7,
        check_vma=False,
    )
```

```python
import functools

import jax
import jax.numpy as jnp
from jax import lax
from jax.experimental import pallas as pl
from jax.experimental.pallas import tpu as pltpu
from jax.sharding import PartitionSpec as P

NS_ITERS = 2
BF16 = jnp.bfloat16
F32 = jnp.float32


def dot(a, b, ca, cb):
    return lax.dot_general(a, b, (((ca,), (cb,)), ((), ())), preferred_element_type=F32)


def pick(array, index, axis):
    return lax.dynamic_index_in_dim(array, index, axis, keepdims=False)


def part(array, index, size, axis):
    return lax.dynamic_slice_in_dim(array, index * size, size, axis)


def later_rows(rows, n_chain):
    return rows // (2 * (n_chain - 1)) // 16 * 16


def chunks(rows):
    count = 4 if rows >= 256 else 2
    units = rows // 16
    sizes = [(units // count + (k < units % count)) * 16 for k in range(count)]
    return [size for size in sizes if size] if rows % 16 == 0 else [rows]


def gather_kernel(n_chain, n_tensor, n_across, n_along, n_swap, pieces, *refs):
    count = n_across + n_along + n_swap
    ins, outs = refs[:count], refs[count : 2 * count]
    local_sem = refs[2 * count]
    sems = refs[2 * count + 1 :]
    s, t = lax.axis_index("shard"), lax.axis_index("tensor")
    a, b = s // 2, s % 2
    pair = (a * 2 + 1 - b, t)
    right = (lax.rem(a + 1, n_chain) * 2 + b, t)
    left = (lax.rem(a + n_chain - 1, n_chain) * 2 + b, t)
    near_t = t + 1 - 2 * (t % 2)
    far_t = lax.rem(t + n_tensor // 2, n_tensor)
    near, far = (s, near_t), (s, far_t)
    others = ([pair, right, left] if n_across else []) + ([near] if n_along else [])
    others += [far] if n_along or n_swap else []
    barrier = pltpu.get_barrier_semaphore()
    for other in others:
        pl.semaphore_signal(barrier, inc=1, device_id=other, device_id_type=pl.DeviceIdType.MESH)
    pl.semaphore_wait(barrier, len(others))

    def remote(src, dst, send_sem, recv_sem, target):
        return pltpu.make_async_remote_copy(
            src_ref=src,
            dst_ref=dst,
            send_sem=send_sem,
            recv_sem=recv_sem,
            device_id=target,
            device_id_type=pl.DeviceIdType.MESH,
        )

    def across(p, block, send, target, own=False):
        i, first, rows, _ = pieces[p]
        dst = outs[i].at[block, pl.ds(first, rows)]
        src = ins[i].at[pl.ds(first, rows)] if own else dst
        return remote(src, dst, sems[2 * p].at[send], sems[2 * p + 1].at[block], target)

    def along(i, block, send, target, own=False):
        pos = 2 * (len(pieces) + i - n_across)
        dst = outs[i].at[block]
        src = ins[i] if own else dst
        return remote(src, dst, sems[pos].at[send], sems[pos + 1].at[block], target)

    def swap(i):
        pos = 2 * (len(pieces) + i - n_across)
        return remote(ins[i], outs[i], sems[pos].at[0], sems[pos + 1].at[0], far)

    has_right, has_left = a + 1 < n_chain, a >= 1
    extra = 2 * n_chain
    order = sorted(range(len(pieces)), key=lambda p: not pieces[p][3])
    for p in order:
        pl.when(has_right)(lambda p=p: across(p, s, a, right, True).start())
        pl.when(has_left)(lambda p=p: across(p, s, extra, left, True).start())
        across(p, s, extra + 2 if pieces[p][3] else n_chain + a, pair, True).start()
    for i in range(n_across, n_across + n_along):
        along(i, t, 0, far, True).start()
        along(i, t, 1, near, True).start()
    for i in range(n_across + n_along, count):
        swap(i).start()
    locals_ = []
    for i in range(n_across + n_along):
        own = pltpu.make_async_copy(ins[i], outs[i].at[s if i < n_across else t], local_sem.at[i])
        own.start()
        locals_.append(own)
    for p in order:
        if pieces[p][3]:
            block = a * 2 + 1 - b
            across(p, block, extra + 2, pair).wait_recv()
            pl.when(has_right)(lambda p=p, block=block: across(p, block, n_chain + a, right).start())
            pl.when(has_left)(lambda p=p, block=block: across(p, block, extra + 1, left).start())

    def step(k, carry):
        for p in order:
            pair_first = pieces[p][3]
            for side in range(2 if pair_first else 1):
                col = 1 - b if side else b

                @pl.when(a - k >= 0)
                def _():
                    block = (a - k) * 2 + col
                    send = side * n_chain + a - k
                    across(p, block, send, right).wait_recv()
                    pl.when(has_right)(lambda: across(p, block, send, right).start())
                    if not pair_first:
                        across(p, block, n_chain + a - k, pair).start()

                @pl.when(a + k < n_chain)
                def _():
                    block = (a + k) * 2 + col
                    send = side * n_chain + a + k
                    across(p, block, send, left).wait_recv()
                    pl.when(has_left)(lambda: across(p, block, send, left).start())
                    if not pair_first:
                        across(p, block, n_chain + a + k, pair).start()

        return carry

    if n_across:
        lax.fori_loop(1, n_chain - 1, step, 0)
    for i in range(n_across, n_across + n_along):
        along(i, far_t, 2, near).wait_recv()
        along(i, far_t, 2, near).start()
    if n_across:
        step(n_chain - 1, 0)

        def finish(j, carry):
            for p in order:
                pair_first = pieces[p][3]
                if not pair_first:
                    across(p, j * 2 + 1 - b, n_chain + j, pair).wait_recv()
                    across(p, j * 2 + b, n_chain + j, pair).wait_send()
                for side in range(2 if pair_first else 1):
                    block = j * 2 + (1 - b if side else b)
                    send = side * n_chain + j
                    pl.when((j <= a) & has_right)(lambda: across(p, block, send, right).wait_send())
                    pl.when((j > a) & has_left)(lambda: across(p, block, send, left).wait_send())
            return carry

        lax.fori_loop(0, n_chain, finish, 0)
        for p in order:
            pl.when(has_left)(lambda p=p: across(p, s, extra, left).wait_send())
            if pieces[p][3]:
                pl.when(has_left)(lambda p=p: across(p, s, extra + 1, left).wait_send())
                across(p, s, extra + 2, pair).wait_send()
    near_far = near_t + far_t - t
    for i in range(n_across, n_across + n_along):
        along(i, near_t, 1, near).wait_recv()
        along(i, near_far, 2, near).wait_recv()
        for send in range(3):
            along(i, t, send, near).wait_send()
    for i in range(n_across + n_along, count):
        swap(i).wait()
    for own in locals_:
        own.wait()


def gather(name, across, along, swaps=(), *, n_shard, n_tensor):
    arrays = list(across) + list(along) + list(swaps)
    pieces = []
    for i, x in enumerate(across):
        later = later_rows(x.shape[0], n_shard // 2)
        main = x.shape[0] - later
        first = 0
        for rows in chunks(main) if later else [main]:
            pieces.append((i, first, rows, False))
            first += rows
        if later:
            pieces.append((i, main, later, True))
    shapes = [(n_shard, *x.shape) for x in across]
    shapes += [(n_tensor, *x.shape) for x in along] + [x.shape for x in swaps]
    counts = [(n_shard + 3, n_shard)] * len(pieces) + [(3, n_tensor)] * len(along) + [(1, 1)] * len(swaps)
    scratch = [pltpu.SemaphoreType.DMA((len(arrays),))]
    for sends, receives in counts:
        scratch += [pltpu.SemaphoreType.DMA((sends,)), pltpu.SemaphoreType.DMA((receives,))]
    return pl.pallas_call(
        functools.partial(
            gather_kernel, n_shard // 2, n_tensor, len(across), len(along), len(swaps), tuple(pieces)
        ),
        out_shape=[jax.ShapeDtypeStruct(shape, x.dtype) for shape, x in zip(shapes, arrays)],
        in_specs=[pl.BlockSpec(memory_space=pl.ANY)] * len(arrays),
        out_specs=[pl.BlockSpec(memory_space=pl.ANY)] * len(arrays),
        scratch_shapes=scratch,
        compiler_params=pltpu.CompilerParams(collective_id=name, has_side_effects=True),
        name="gather",
    )(*arrays)


def side_by_side(blocks):
    n, rows, cols = blocks.shape
    return blocks.transpose(1, 0, 2).reshape(rows, n * cols)


def stacked(blocks):
    return blocks.reshape(-1, blocks.shape[-1])


def lanes(array):
    return array.reshape(-1, 128)


def swap(array, bit, n_tensor):
    return lax.ppermute(array, "tensor", [(i, i ^ bit) for i in range(n_tensor)])


def gram_half(rows, panel, core, n_tensor):
    half = panel.shape[0] // 2
    other = dot(rows, part(panel, 1 - core, half, 0), 1, 1).astype(BF16)
    other = swap(other, 1, n_tensor)
    return dot(rows, part(panel, core, half, 0), 1, 1) + other.astype(F32)


def apply_gram(halves, panel, core):
    mine, other = halves
    half = mine.shape[1]
    return dot(mine, part(panel, core, half, 0), 1, 0) + dot(
        other, part(panel, 1 - core, half, 0), 1, 0
    )


def scatter_sum(terms, t, n_tensor):
    rows = terms.shape[0]
    width = terms.shape[1] // n_tensor
    terms = terms.reshape(rows, n_tensor // 2, 2, width)
    core = t % 2
    mine = pick(terms, core, 2) + swap(pick(terms, 1 - core, 2), 1, n_tensor)
    pair = t // 2
    count = n_tensor // 2
    while count > 1:
        count //= 2
        mine = mine.reshape(rows, 2, count, width)
        bit = (pair // count) % 2
        mine = pick(mine, bit, 1) + swap(pick(mine, 1 - bit, 1), 2 * count, n_tensor)
    return mine.reshape(rows, width)


def whole_sum(value, n_tensor):
    bit = 1
    while bit < n_tensor:
        value = value + swap(value, bit, n_tensor)
        bit *= 2
    return value


def make(n_shard, n_tensor):
    def per_device(gradient, moment, second_moment, stat_left, stat_right, basis_left, basis_right):
        s = lax.axis_index("shard")
        t = lax.axis_index("tensor")
        core = t % 2
        rows_left, block_hidden = gradient.shape
        rows_right = stat_right.shape[0]
        block_left = stat_left.shape[1]
        run = functools.partial(gather, n_shard=n_shard, n_tensor=n_tensor)

        moment_new = 0.9 * moment + 0.1 * gradient.astype(F32)
        third = rows_right // 3
        thirds = [part(basis_right, k, third, 0).astype(BF16) for k in range(3)]
        panel, left_blocks, right_0, grad_rows, moment_rows = run(
            0,
            [gradient, lanes(basis_left.astype(BF16)), thirds[0]],
            [gradient, moment_new.astype(BF16)],
        )
        panel = stacked(panel)
        first = s * rows_right
        owner = first // block_hidden
        strip = lax.dynamic_slice_in_dim(panel, first - owner * block_hidden, rows_right, 1)
        right_1, strips = run(1, [thirds[1]], [strip])
        strip = pick(strips, owner, 0)
        stat_right_new = 0.95 * stat_right + 0.05 * dot(strip, panel, 0, 0)
        cross_left = scatter_sum(dot(gradient, panel, 1, 1), t, n_tensor)
        stat_left_new = 0.95 * stat_left + 0.05 * cross_left
        right_2, stat_left_columns, stat_right_rows, left = run(
            2,
            [thirds[2], lanes(stat_left_new.astype(BF16))],
            [stat_right_new.astype(BF16), lanes(left_blocks.reshape(-1, block_left))],
        )
        left = side_by_side(left.reshape(n_tensor, n_shard * rows_left, block_left))
        right_columns = stacked(jnp.concatenate([right_0, right_1, right_2], axis=1))

        power = dot(side_by_side(stat_right_rows), right_columns, 1, 0)
        power_half = power.astype(BF16)
        square = jnp.full((8, 128), jnp.sum(power * power), F32)
        rotated = jnp.concatenate([side_by_side(grad_rows), side_by_side(moment_rows)])
        rotated = dot(rotated, right_columns, 1, 0).astype(BF16)
        grad_right, moment_right = rotated[:rows_left], rotated[rows_left:]
        power_panel, squares = run(3, [power_half, square], [])
        power_panel = stacked(power_panel)

        square = whole_sum(jnp.sum(squares[:, 0, 0]), n_tensor)
        scale = 1.0 / jnp.sqrt(square + 1e-06)
        mine = gram_half(power_half, power_panel, core, n_tensor)
        grad_right, moment_right, there = run(4, [grad_right, moment_right], [], [mine.astype(BF16)])
        mine = (((mine + there.astype(F32)) * scale) * scale).astype(BF16)
        halves = mine, swap(mine, 1, n_tensor)
        iterate = scale * (1.5 * power - 0.5 * apply_gram(halves, power_panel, core))

        basis_strip = part(left, s, rows_left, 1)
        grad_turned = dot(basis_strip, stacked(grad_right), 0, 0)
        moment_turned = dot(basis_strip, stacked(moment_right), 0, 0)
        second_new = 0.95 * second_moment + 0.05 * grad_turned * grad_turned
        scaled = (moment_turned / (jnp.sqrt(second_new) + 1e-08)).astype(BF16)
        back_half = scatter_sum(dot(scaled, right_columns, 1, 1), t, n_tensor).astype(BF16)

        def left_basis(stat_left_all):
            stat_all = side_by_side(stat_left_all.reshape(n_tensor, n_shard * rows_left, block_left))
            power_left = dot(stat_all, left, 1, 0)
            iterate_left = power_left / jnp.sqrt(jnp.sum(power_left * power_left) + 1e-06)
            for step in range(NS_ITERS):
                left_half = iterate_left.astype(BF16)
                if step < NS_ITERS - 1:
                    gram = dot(left_half, left_half, 1, 1).astype(BF16)
                    iterate_left = 1.5 * iterate_left - 0.5 * dot(gram, left_half, 1, 0)
                else:
                    gram = dot(part(left_half, s, rows_left, 0), left_half, 1, 1).astype(BF16)
                    own = part(part(iterate_left, s, rows_left, 0), t, block_left, 1)
                    iterate_left = 1.5 * own - 0.5 * dot(gram, part(left_half, t, block_left, 1), 1, 0)
            return iterate_left

        def gram_whole(mine, there):
            mine = (mine + there.astype(F32)).astype(BF16)
            return mine, swap(mine, 1, n_tensor)

        update = None
        for step in range(NS_ITERS - 1):
            iterate_half = iterate.astype(BF16)
            upper, lower = jnp.split(iterate_half, 2)
            (upper,) = run(5 + 2 * step, [upper], [])
            upper = stacked(upper)
            mine_upper = gram_half(iterate_half, upper, core, n_tensor)
            if step == 0:
                lower, back_panel, stat_left_all, there_upper = run(
                    6, [lower, back_half], [lanes(stat_left_columns.reshape(-1, 128))], [mine_upper.astype(BF16)]
                )
                update = dot(part(left, s, rows_left, 0), stacked(back_panel), 1, 0)
            else:
                lower, there_upper = run(6 + 2 * step, [lower], [], [mine_upper.astype(BF16)])
            lower = stacked(lower)
            mine_lower = gram_half(iterate_half, lower, core, n_tensor)
            there_lower = swap(mine_lower.astype(BF16), n_tensor // 2, n_tensor)
            halves = gram_whole(mine_upper, there_upper)
            change = apply_gram(halves, upper, core)
            if step == NS_ITERS - 2:
                there_lower, iterate_left, update, change = lax.optimization_barrier(
                    (there_lower, left_basis(stat_left_all), update, change)
                )
            change = change + apply_gram(gram_whole(mine_lower, there_lower), lower, core)
            iterate = 1.5 * iterate - 0.5 * change

        return (
            update,
            moment_new,
            second_new,
            stat_left_new,
            stat_right_new,
            iterate_left,
            iterate,
        )

    return per_device


def solution(mesh):
    spec = P("shard", "tensor")
    return jax.shard_map(
        make(mesh.shape["shard"], mesh.shape["tensor"]),
        mesh=mesh,
        in_specs=(spec,) * 7,
        out_specs=(spec,) * 7,
        check_vma=False,
    )
```

```python
import functools

import jax
import jax.numpy as jnp
from jax import lax
from jax.experimental import pallas as pl
from jax.experimental.pallas import tpu as pltpu
from jax.sharding import PartitionSpec as P

NS_ITERS = 2
BF16 = jnp.bfloat16
F32 = jnp.float32


def dot(a, b, ca, cb):
    return lax.dot_general(a, b, (((ca,), (cb,)), ((), ())), preferred_element_type=F32)


def pick(array, index, axis):
    return lax.dynamic_index_in_dim(array, index, axis, keepdims=False)


def part(array, index, size, axis):
    return lax.dynamic_slice_in_dim(array, index * size, size, axis)


def later_rows(rows, n_chain):
    return rows // (2 * (n_chain - 1)) // 16 * 16


def chunks(rows):
    count = 4 if rows >= 256 else 2
    units = rows // 16
    sizes = [(units // count + (k < units % count)) * 16 for k in range(count)]
    return [size for size in sizes if size] if rows % 16 == 0 else [rows]


def gather_kernel(n_chain, n_tensor, n_across, n_along, n_swap, n_cast, cast_ratio, pieces, *refs):
    count = n_across + n_along + n_swap + n_cast
    ins, outs = refs[:count], refs[count : 2 * count]
    local_sem = refs[2 * count]
    sems = refs[2 * count + 1 :]
    s, t = lax.axis_index("shard"), lax.axis_index("tensor")
    a, b = s // 2, s % 2
    pair = (a * 2 + 1 - b, t)
    right = (lax.rem(a + 1, n_chain) * 2 + b, t)
    left = (lax.rem(a + n_chain - 1, n_chain) * 2 + b, t)
    near_t = t + 1 - 2 * (t % 2)
    far_t = lax.rem(t + n_tensor // 2, n_tensor)
    near, far = (s, near_t), (s, far_t)
    others = ([pair, right, left] if n_across else []) + ([near] if n_along or n_cast else [])
    others += [far] if n_along or n_swap or n_cast else []
    barrier = pltpu.get_barrier_semaphore()
    for other in others:
        pl.semaphore_signal(barrier, inc=1, device_id=other, device_id_type=pl.DeviceIdType.MESH)
    pl.semaphore_wait(barrier, len(others))

    def remote(src, dst, send_sem, recv_sem, target):
        return pltpu.make_async_remote_copy(
            src_ref=src,
            dst_ref=dst,
            send_sem=send_sem,
            recv_sem=recv_sem,
            device_id=target,
            device_id_type=pl.DeviceIdType.MESH,
        )

    def across(p, block, send, target, own=False):
        i, first, rows, _ = pieces[p]
        dst = outs[i].at[block, pl.ds(first, rows)]
        src = ins[i].at[pl.ds(first, rows)] if own else dst
        return remote(src, dst, sems[2 * p].at[send], sems[2 * p + 1].at[block], target)

    def along(i, block, send, target, own=False):
        pos = 2 * (len(pieces) + i - n_across)
        dst = outs[i].at[block]
        src = ins[i] if own else dst
        return remote(src, dst, sems[pos].at[send], sems[pos + 1].at[block], target)

    def swap(i):
        pos = 2 * (len(pieces) + i - n_across)
        return remote(ins[i], outs[i], sems[pos].at[0], sems[pos + 1].at[0], far)

    owner = (s * cast_ratio[0]) // cast_ratio[1]
    is_owner, is_far = t == owner, far_t == owner
    is_other = (near_t == owner) | (near_t + far_t - t == owner)

    def cast(i, send, target, own=False):
        pos = 2 * (len(pieces) + i - n_across)
        return remote(ins[i] if own else outs[i], outs[i], sems[pos].at[send], sems[pos + 1].at[0], target)

    def keep(i):
        return pltpu.make_async_copy(ins[i], outs[i], local_sem.at[i])

    has_right, has_left = a + 1 < n_chain, a >= 1
    extra = 2 * n_chain
    order = sorted(range(len(pieces)), key=lambda p: not pieces[p][3])
    for p in order:
        pl.when(has_right)(lambda p=p: across(p, s, a, right, True).start())
        pl.when(has_left)(lambda p=p: across(p, s, extra, left, True).start())
        across(p, s, extra + 2 if pieces[p][3] else n_chain + a, pair, True).start()
    for i in range(n_across, n_across + n_along):
        along(i, t, 0, far, True).start()
        along(i, t, 1, near, True).start()
    n_gathered = n_across + n_along
    for i in range(n_gathered, n_gathered + n_swap):
        swap(i).start()
    for i in range(n_gathered + n_swap, count):

        @pl.when(is_owner)
        def _():
            cast(i, 0, far, True).start()
            cast(i, 1, near, True).start()
            keep(i).start()

    locals_ = []
    for i in range(n_across + n_along):
        own = pltpu.make_async_copy(ins[i], outs[i].at[s if i < n_across else t], local_sem.at[i])
        own.start()
        locals_.append(own)
    for p in order:
        if pieces[p][3]:
            block = a * 2 + 1 - b
            across(p, block, extra + 2, pair).wait_recv()
            pl.when(has_right)(lambda p=p, block=block: across(p, block, n_chain + a, right).start())
            pl.when(has_left)(lambda p=p, block=block: across(p, block, extra + 1, left).start())

    def step(k, carry):
        for p in order:
            pair_first = pieces[p][3]
            for side in range(2 if pair_first else 1):
                col = 1 - b if side else b

                @pl.when(a - k >= 0)
                def _():
                    block = (a - k) * 2 + col
                    send = side * n_chain + a - k
                    across(p, block, send, right).wait_recv()
                    pl.when(has_right)(lambda: across(p, block, send, right).start())
                    if not pair_first:
                        across(p, block, n_chain + a - k, pair).start()

                @pl.when(a + k < n_chain)
                def _():
                    block = (a + k) * 2 + col
                    send = side * n_chain + a + k
                    across(p, block, send, left).wait_recv()
                    pl.when(has_left)(lambda: across(p, block, send, left).start())
                    if not pair_first:
                        across(p, block, n_chain + a + k, pair).start()

        return carry

    if n_across:
        lax.fori_loop(1, n_chain - 1, step, 0)
    for i in range(n_across, n_across + n_along):
        along(i, far_t, 2, near).wait_recv()
        along(i, far_t, 2, near).start()
    for i in range(n_gathered + n_swap, count):

        @pl.when(is_far)
        def _():
            cast(i, 0, near).wait_recv()
            cast(i, 0, near).start()

    if n_across:
        step(n_chain - 1, 0)

        def finish(j, carry):
            for p in order:
                pair_first = pieces[p][3]
                if not pair_first:
                    across(p, j * 2 + 1 - b, n_chain + j, pair).wait_recv()
                    across(p, j * 2 + b, n_chain + j, pair).wait_send()
                for side in range(2 if pair_first else 1):
                    block = j * 2 + (1 - b if side else b)
                    send = side * n_chain + j
                    pl.when((j <= a) & has_right)(lambda: across(p, block, send, right).wait_send())
                    pl.when((j > a) & has_left)(lambda: across(p, block, send, left).wait_send())
            return carry

        lax.fori_loop(0, n_chain, finish, 0)
        for p in order:
            pl.when(has_left)(lambda p=p: across(p, s, extra, left).wait_send())
            if pieces[p][3]:
                pl.when(has_left)(lambda p=p: across(p, s, extra + 1, left).wait_send())
                across(p, s, extra + 2, pair).wait_send()
    near_far = near_t + far_t - t
    for i in range(n_across, n_across + n_along):
        along(i, near_t, 1, near).wait_recv()
        along(i, near_far, 2, near).wait_recv()
        for send in range(3):
            along(i, t, send, near).wait_send()
    for i in range(n_gathered, n_gathered + n_swap):
        swap(i).wait()
    for i in range(n_gathered + n_swap, count):
        pl.when(is_other)(lambda i=i: cast(i, 0, near).wait_recv())
        pl.when(is_far)(lambda i=i: cast(i, 0, near).wait_send())

        @pl.when(is_owner)
        def _():
            cast(i, 0, far, True).wait_send()
            cast(i, 1, near, True).wait_send()
            keep(i).wait()

    for own in locals_:
        own.wait()


def gather(name, across, along, swaps=(), casts=(), cast_ratio=(0, 1), *, n_shard, n_tensor):
    arrays = list(across) + list(along) + list(swaps) + list(casts)
    pieces = []
    for i, x in enumerate(across):
        later = later_rows(x.shape[0], n_shard // 2)
        main = x.shape[0] - later
        first = 0
        for rows in chunks(main) if later else [main]:
            pieces.append((i, first, rows, False))
            first += rows
        if later:
            pieces.append((i, main, later, True))
    shapes = [(n_shard, *x.shape) for x in across]
    shapes += [(n_tensor, *x.shape) for x in along] + [x.shape for x in [*swaps, *casts]]
    counts = [(n_shard + 3, n_shard)] * len(pieces) + [(3, n_tensor)] * len(along) + [(1, 1)] * len(swaps)
    counts += [(2, 1)] * len(casts)
    scratch = [pltpu.SemaphoreType.DMA((len(arrays),))]
    for sends, receives in counts:
        scratch += [pltpu.SemaphoreType.DMA((sends,)), pltpu.SemaphoreType.DMA((receives,))]
    return pl.pallas_call(
        functools.partial(
            gather_kernel,
            n_shard // 2,
            n_tensor,
            len(across),
            len(along),
            len(swaps),
            len(casts),
            cast_ratio,
            tuple(pieces),
        ),
        out_shape=[jax.ShapeDtypeStruct(shape, x.dtype) for shape, x in zip(shapes, arrays)],
        in_specs=[pl.BlockSpec(memory_space=pl.ANY)] * len(arrays),
        out_specs=[pl.BlockSpec(memory_space=pl.ANY)] * len(arrays),
        scratch_shapes=scratch,
        compiler_params=pltpu.CompilerParams(collective_id=name, has_side_effects=True),
        name="gather",
    )(*arrays)


def side_by_side(blocks):
    n, rows, cols = blocks.shape
    return blocks.transpose(1, 0, 2).reshape(rows, n * cols)


def stacked(blocks):
    return blocks.reshape(-1, blocks.shape[-1])


def lanes(array):
    return array.reshape(-1, 128)


def swap(array, bit, n_tensor):
    return lax.ppermute(array, "tensor", [(i, i ^ bit) for i in range(n_tensor)])


def gram_half(rows, panel, core, n_tensor):
    half = panel.shape[0] // 2
    other = dot(rows, part(panel, 1 - core, half, 0), 1, 1).astype(BF16)
    other = swap(other, 1, n_tensor)
    return dot(rows, part(panel, core, half, 0), 1, 1) + other.astype(F32)


def apply_gram(halves, panel, core):
    mine, other = halves
    half = mine.shape[1]
    return dot(mine, part(panel, core, half, 0), 1, 0) + dot(
        other, part(panel, 1 - core, half, 0), 1, 0
    )


def scatter_sum(terms, t, n_tensor):
    rows = terms.shape[0]
    width = terms.shape[1] // n_tensor
    terms = terms.reshape(rows, n_tensor // 2, 2, width)
    core = t % 2
    mine = pick(terms, core, 2) + swap(pick(terms, 1 - core, 2), 1, n_tensor)
    pair = t // 2
    count = n_tensor // 2
    while count > 1:
        count //= 2
        mine = mine.reshape(rows, 2, count, width)
        bit = (pair // count) % 2
        mine = pick(mine, bit, 1) + swap(pick(mine, 1 - bit, 1), 2 * count, n_tensor)
    return mine.reshape(rows, width)


def whole_sum(value, n_tensor):
    bit = 1
    while bit < n_tensor:
        value = value + swap(value, bit, n_tensor)
        bit *= 2
    return value


def make(n_shard, n_tensor):
    def per_device(gradient, moment, second_moment, stat_left, stat_right, basis_left, basis_right):
        s = lax.axis_index("shard")
        t = lax.axis_index("tensor")
        core = t % 2
        rows_left, block_hidden = gradient.shape
        rows_right = stat_right.shape[0]
        block_left = stat_left.shape[1]
        run = functools.partial(gather, n_shard=n_shard, n_tensor=n_tensor)

        moment_new = 0.9 * moment + 0.1 * gradient.astype(F32)
        third = rows_right // 3
        thirds = [part(basis_right, k, third, 0).astype(BF16) for k in range(3)]
        panel, left_blocks, right_0, grad_rows, moment_rows = run(
            0,
            [gradient, lanes(basis_left.astype(BF16)), thirds[0]],
            [gradient, moment_new.astype(BF16)],
        )
        panel = stacked(panel)
        first = s * rows_right
        owner = first // block_hidden
        strip = lax.dynamic_slice_in_dim(panel, first - owner * block_hidden, rows_right, 1)
        right_1, left, strip = run(
            1,
            [thirds[1]],
            [lanes(left_blocks.reshape(-1, block_left))],
            casts=[strip],
            cast_ratio=(rows_right, block_hidden),
        )
        stat_right_new = 0.95 * stat_right + 0.05 * dot(strip, panel, 0, 0)
        cross_left = scatter_sum(dot(gradient, panel, 1, 1), t, n_tensor)
        stat_left_new = 0.95 * stat_left + 0.05 * cross_left
        right_2, stat_left_columns, stat_right_rows = run(
            2, [thirds[2], lanes(stat_left_new.astype(BF16))], [stat_right_new.astype(BF16)]
        )
        left = side_by_side(left.reshape(n_tensor, n_shard * rows_left, block_left))
        right_columns = stacked(jnp.concatenate([right_0, right_1, right_2], axis=1))

        power = dot(side_by_side(stat_right_rows), right_columns, 1, 0)
        power_half = power.astype(BF16)
        square = jnp.full((8, 128), jnp.sum(power * power), F32)
        rotated = jnp.concatenate([side_by_side(grad_rows), side_by_side(moment_rows)])
        rotated = dot(rotated, right_columns, 1, 0).astype(BF16)
        grad_right, moment_right = rotated[:rows_left], rotated[rows_left:]
        power_panel, squares = run(3, [power_half, square], [])
        power_panel = stacked(power_panel)

        square = whole_sum(jnp.sum(squares[:, 0, 0]), n_tensor)
        scale = 1.0 / jnp.sqrt(square + 1e-06)
        mine = gram_half(power_half, power_panel, core, n_tensor)
        grad_right, moment_right, there = run(4, [grad_right, moment_right], [], [mine.astype(BF16)])
        mine = (((mine + there.astype(F32)) * scale) * scale).astype(BF16)
        halves = mine, swap(mine, 1, n_tensor)
        iterate = scale * (1.5 * power - 0.5 * apply_gram(halves, power_panel, core))

        basis_strip = part(left, s, rows_left, 1)
        grad_turned = dot(basis_strip, stacked(grad_right), 0, 0)
        moment_turned = dot(basis_strip, stacked(moment_right), 0, 0)
        second_new = 0.95 * second_moment + 0.05 * grad_turned * grad_turned
        scaled = (moment_turned / (jnp.sqrt(second_new) + 1e-08)).astype(BF16)
        terms = dot(scaled, right_columns, 1, 1).reshape(rows_left, n_tensor // 2, 2, block_hidden)
        terms = pick(terms, core, 2) + swap(pick(terms, 1 - core, 2), 1, n_tensor)
        back = pick(terms, t // 2, 1)

        def left_basis(stat_left_all):
            stat_all = side_by_side(stat_left_all.reshape(n_tensor, n_shard * rows_left, block_left))
            power_left = dot(stat_all, left, 1, 0)
            iterate_left = power_left / jnp.sqrt(jnp.sum(power_left * power_left) + 1e-06)
            for step in range(NS_ITERS):
                left_half = iterate_left.astype(BF16)
                if step < NS_ITERS - 1:
                    gram = dot(left_half, left_half, 1, 1).astype(BF16)
                    iterate_left = 1.5 * iterate_left - 0.5 * dot(gram, left_half, 1, 0)
                else:
                    gram = dot(part(left_half, s, rows_left, 0), left_half, 1, 1).astype(BF16)
                    own = part(part(iterate_left, s, rows_left, 0), t, block_left, 1)
                    iterate_left = 1.5 * own - 0.5 * dot(gram, part(left_half, t, block_left, 1), 1, 0)
            return iterate_left

        def gram_whole(mine, there):
            mine = (mine + there.astype(F32)).astype(BF16)
            return mine, swap(mine, 1, n_tensor)

        update = None
        for step in range(NS_ITERS - 1):
            iterate_half = iterate.astype(BF16)
            upper, lower = jnp.split(iterate_half, 2)
            if step == 0:
                upper, back_there = run(5, [upper], [], [pick(terms, 1 - t // 2, 1)])
                back_half = (back + back_there).astype(BF16)
            else:
                (upper,) = run(5 + 2 * step, [upper], [])
            upper = stacked(upper)
            mine_upper = gram_half(iterate_half, upper, core, n_tensor)
            if step == 0:
                lower, back_panel, stat_left_all, there_upper = run(
                    6, [lower, back_half], [lanes(stat_left_columns.reshape(-1, 128))], [mine_upper.astype(BF16)]
                )
                update = dot(part(left, s, rows_left, 0), stacked(back_panel), 1, 0)
            else:
                lower, there_upper = run(6 + 2 * step, [lower], [], [mine_upper.astype(BF16)])
            lower = stacked(lower)
            mine_lower = gram_half(iterate_half, lower, core, n_tensor)
            if step == NS_ITERS - 2:
                mine_lower, stat_left_all = lax.optimization_barrier((mine_lower, stat_left_all))
            there_lower = swap(mine_lower.astype(BF16), n_tensor // 2, n_tensor)
            halves = gram_whole(mine_upper, there_upper)
            change = apply_gram(halves, upper, core)
            if step == NS_ITERS - 2:
                there_lower, iterate_left, update, change = lax.optimization_barrier(
                    (there_lower, left_basis(stat_left_all), update, change)
                )
            change = change + apply_gram(gram_whole(mine_lower, there_lower), lower, core)
            iterate = 1.5 * iterate - 0.5 * change

        return (
            update,
            moment_new,
            second_new,
            stat_left_new,
            stat_right_new,
            iterate_left,
            iterate,
        )

    return per_device


def solution(mesh):
    spec = P("shard", "tensor")
    return jax.shard_map(
        make(mesh.shape["shard"], mesh.shape["tensor"]),
        mesh=mesh,
        in_specs=(spec,) * 7,
        out_specs=(spec,) * 7,
        check_vma=False,
    )
```

```python
import functools

import jax
import jax.numpy as jnp
from jax import lax
from jax.experimental import pallas as pl
from jax.experimental.pallas import tpu as pltpu
from jax.sharding import PartitionSpec as P

NS_ITERS = 2
BF16 = jnp.bfloat16
F32 = jnp.float32


def dot(a, b, ca, cb):
    return lax.dot_general(a, b, (((ca,), (cb,)), ((), ())), preferred_element_type=F32)


def pick(array, index, axis):
    return lax.dynamic_index_in_dim(array, index, axis, keepdims=False)


def part(array, index, size, axis):
    return lax.dynamic_slice_in_dim(array, index * size, size, axis)


def later_rows(rows, n_chain):
    return rows // (2 * (n_chain - 1)) // 16 * 16


def chunks(rows):
    count = 4 if rows >= 256 else 2
    units = rows // 16
    sizes = [(units // count + (k < units % count)) * 16 for k in range(count)]
    return [size for size in sizes if size] if rows % 16 == 0 else [rows]


def gather_kernel(n_chain, n_tensor, n_across, n_along, n_swap, n_cast, cast_ratio, pieces, *refs):
    count = n_across + n_along + n_swap + n_cast
    ins, outs = refs[:count], refs[count : 2 * count]
    local_sem = refs[2 * count]
    sems = refs[2 * count + 1 :]
    s, t = lax.axis_index("shard"), lax.axis_index("tensor")
    a, b = s // 2, s % 2
    pair = (a * 2 + 1 - b, t)
    right = (lax.rem(a + 1, n_chain) * 2 + b, t)
    left = (lax.rem(a + n_chain - 1, n_chain) * 2 + b, t)
    near_t = t + 1 - 2 * (t % 2)
    far_t = lax.rem(t + n_tensor // 2, n_tensor)
    near, far = (s, near_t), (s, far_t)
    others = ([pair, right, left] if n_across else []) + ([near] if n_along or n_cast else [])
    others += [far] if n_along or n_swap or n_cast else []
    barrier = pltpu.get_barrier_semaphore()
    for other in others:
        pl.semaphore_signal(barrier, inc=1, device_id=other, device_id_type=pl.DeviceIdType.MESH)
    pl.semaphore_wait(barrier, len(others))

    def remote(src, dst, send_sem, recv_sem, target):
        return pltpu.make_async_remote_copy(
            src_ref=src,
            dst_ref=dst,
            send_sem=send_sem,
            recv_sem=recv_sem,
            device_id=target,
            device_id_type=pl.DeviceIdType.MESH,
        )

    def across(p, block, send, target, own=False):
        i, first, rows, _ = pieces[p]
        dst = outs[i].at[block, pl.ds(first, rows)]
        src = ins[i].at[pl.ds(first, rows)] if own else dst
        return remote(src, dst, sems[2 * p].at[send], sems[2 * p + 1].at[block], target)

    def along(i, block, send, target, own=False):
        pos = 2 * (len(pieces) + i - n_across)
        dst = outs[i].at[block]
        src = ins[i] if own else dst
        return remote(src, dst, sems[pos].at[send], sems[pos + 1].at[block], target)

    def swap(i):
        pos = 2 * (len(pieces) + i - n_across)
        return remote(ins[i], outs[i], sems[pos].at[0], sems[pos + 1].at[0], far)

    owner = (s * cast_ratio[0]) // cast_ratio[1]
    is_owner, is_far = t == owner, far_t == owner
    is_other = (near_t == owner) | (near_t + far_t - t == owner)

    def cast(i, send, target, own=False):
        pos = 2 * (len(pieces) + i - n_across)
        return remote(ins[i] if own else outs[i], outs[i], sems[pos].at[send], sems[pos + 1].at[0], target)

    def keep(i):
        return pltpu.make_async_copy(ins[i], outs[i], local_sem.at[i])

    has_right, has_left = a + 1 < n_chain, a >= 1
    extra = 2 * n_chain
    order = sorted(range(len(pieces)), key=lambda p: not pieces[p][3])
    for p in order:
        pl.when(has_right)(lambda p=p: across(p, s, a, right, True).start())
        pl.when(has_left)(lambda p=p: across(p, s, extra, left, True).start())
        across(p, s, extra + 2 if pieces[p][3] else n_chain + a, pair, True).start()
    for i in range(n_across, n_across + n_along):
        along(i, t, 0, far, True).start()
        along(i, t, 1, near, True).start()
    n_gathered = n_across + n_along
    for i in range(n_gathered, n_gathered + n_swap):
        swap(i).start()
    for i in range(n_gathered + n_swap, count):

        @pl.when(is_owner)
        def _():
            cast(i, 0, far, True).start()
            cast(i, 1, near, True).start()
            keep(i).start()

    locals_ = []
    for i in range(n_across + n_along):
        own = pltpu.make_async_copy(ins[i], outs[i].at[s if i < n_across else t], local_sem.at[i])
        own.start()
        locals_.append(own)
    for p in order:
        if pieces[p][3]:
            block = a * 2 + 1 - b
            across(p, block, extra + 2, pair).wait_recv()
            pl.when(has_right)(lambda p=p, block=block: across(p, block, n_chain + a, right).start())
            pl.when(has_left)(lambda p=p, block=block: across(p, block, extra + 1, left).start())

    def step(k, carry):
        for p in order:
            pair_first = pieces[p][3]
            for side in range(2 if pair_first else 1):
                col = 1 - b if side else b

                @pl.when(a - k >= 0)
                def _():
                    block = (a - k) * 2 + col
                    send = side * n_chain + a - k
                    across(p, block, send, right).wait_recv()
                    pl.when(has_right)(lambda: across(p, block, send, right).start())
                    if not pair_first:
                        across(p, block, n_chain + a - k, pair).start()

                @pl.when(a + k < n_chain)
                def _():
                    block = (a + k) * 2 + col
                    send = side * n_chain + a + k
                    across(p, block, send, left).wait_recv()
                    pl.when(has_left)(lambda: across(p, block, send, left).start())
                    if not pair_first:
                        across(p, block, n_chain + a + k, pair).start()

        return carry

    if n_across:
        lax.fori_loop(1, n_chain - 1, step, 0)
    for i in range(n_across, n_across + n_along):
        along(i, far_t, 2, near).wait_recv()
        along(i, far_t, 2, near).start()
    for i in range(n_gathered + n_swap, count):

        @pl.when(is_far)
        def _():
            cast(i, 0, near).wait_recv()
            cast(i, 0, near).start()

    if n_across:
        step(n_chain - 1, 0)

        def finish(j, carry):
            for p in order:
                pair_first = pieces[p][3]
                if not pair_first:
                    across(p, j * 2 + 1 - b, n_chain + j, pair).wait_recv()
                    across(p, j * 2 + b, n_chain + j, pair).wait_send()
                for side in range(2 if pair_first else 1):
                    block = j * 2 + (1 - b if side else b)
                    send = side * n_chain + j
                    pl.when((j <= a) & has_right)(lambda: across(p, block, send, right).wait_send())
                    pl.when((j > a) & has_left)(lambda: across(p, block, send, left).wait_send())
            return carry

        lax.fori_loop(0, n_chain, finish, 0)
        for p in order:
            pl.when(has_left)(lambda p=p: across(p, s, extra, left).wait_send())
            if pieces[p][3]:
                pl.when(has_left)(lambda p=p: across(p, s, extra + 1, left).wait_send())
                across(p, s, extra + 2, pair).wait_send()
    near_far = near_t + far_t - t
    for i in range(n_across, n_across + n_along):
        along(i, near_t, 1, near).wait_recv()
        along(i, near_far, 2, near).wait_recv()
        for send in range(3):
            along(i, t, send, near).wait_send()
    for i in range(n_gathered, n_gathered + n_swap):
        swap(i).wait()
    for i in range(n_gathered + n_swap, count):
        pl.when(is_other)(lambda i=i: cast(i, 0, near).wait_recv())
        pl.when(is_far)(lambda i=i: cast(i, 0, near).wait_send())

        @pl.when(is_owner)
        def _():
            cast(i, 0, far, True).wait_send()
            cast(i, 1, near, True).wait_send()
            keep(i).wait()

    for own in locals_:
        own.wait()


def gather(name, across, along, swaps=(), casts=(), cast_ratio=(0, 1), *, n_shard, n_tensor):
    arrays = list(across) + list(along) + list(swaps) + list(casts)
    pieces = []
    for i, x in enumerate(across):
        later = later_rows(x.shape[0], n_shard // 2)
        main = x.shape[0] - later
        first = 0
        for rows in chunks(main) if later else [main]:
            pieces.append((i, first, rows, False))
            first += rows
        if later:
            pieces.append((i, main, later, True))
    shapes = [(n_shard, *x.shape) for x in across]
    shapes += [(n_tensor, *x.shape) for x in along] + [x.shape for x in [*swaps, *casts]]
    counts = [(n_shard + 3, n_shard)] * len(pieces) + [(3, n_tensor)] * len(along) + [(1, 1)] * len(swaps)
    counts += [(2, 1)] * len(casts)
    scratch = [pltpu.SemaphoreType.DMA((len(arrays),))]
    for sends, receives in counts:
        scratch += [pltpu.SemaphoreType.DMA((sends,)), pltpu.SemaphoreType.DMA((receives,))]
    return pl.pallas_call(
        functools.partial(
            gather_kernel,
            n_shard // 2,
            n_tensor,
            len(across),
            len(along),
            len(swaps),
            len(casts),
            cast_ratio,
            tuple(pieces),
        ),
        out_shape=[jax.ShapeDtypeStruct(shape, x.dtype) for shape, x in zip(shapes, arrays)],
        in_specs=[pl.BlockSpec(memory_space=pl.ANY)] * len(arrays),
        out_specs=[pl.BlockSpec(memory_space=pl.ANY)] * len(arrays),
        scratch_shapes=scratch,
        compiler_params=pltpu.CompilerParams(collective_id=name, has_side_effects=True),
        name="gather",
    )(*arrays)


def side_by_side(blocks):
    n, rows, cols = blocks.shape
    return blocks.transpose(1, 0, 2).reshape(rows, n * cols)


def stacked(blocks):
    return blocks.reshape(-1, blocks.shape[-1])


def lanes(array):
    return array.reshape(-1, 128)


def swap(array, bit, n_tensor):
    return lax.ppermute(array, "tensor", [(i, i ^ bit) for i in range(n_tensor)])


def gram_half(rows, panel, core, n_tensor):
    half = panel.shape[0] // 2
    other = dot(rows, part(panel, 1 - core, half, 0), 1, 1).astype(BF16)
    other = swap(other, 1, n_tensor)
    return dot(rows, part(panel, core, half, 0), 1, 1) + other.astype(F32)


def apply_gram(halves, panel, core):
    mine, other = halves
    half = mine.shape[1]
    return dot(mine, part(panel, core, half, 0), 1, 0) + dot(
        other, part(panel, 1 - core, half, 0), 1, 0
    )


def scatter_sum(terms, t, n_tensor):
    rows = terms.shape[0]
    width = terms.shape[1] // n_tensor
    terms = terms.reshape(rows, n_tensor // 2, 2, width)
    core = t % 2
    mine = pick(terms, core, 2) + swap(pick(terms, 1 - core, 2), 1, n_tensor)
    pair = t // 2
    count = n_tensor // 2
    while count > 1:
        count //= 2
        mine = mine.reshape(rows, 2, count, width)
        bit = (pair // count) % 2
        mine = pick(mine, bit, 1) + swap(pick(mine, 1 - bit, 1), 2 * count, n_tensor)
    return mine.reshape(rows, width)


def whole_sum(value, n_tensor):
    bit = 1
    while bit < n_tensor:
        value = value + swap(value, bit, n_tensor)
        bit *= 2
    return value


def make(n_shard, n_tensor):
    def per_device(gradient, moment, second_moment, stat_left, stat_right, basis_left, basis_right):
        s = lax.axis_index("shard")
        t = lax.axis_index("tensor")
        core = t % 2
        rows_left, block_hidden = gradient.shape
        rows_right = stat_right.shape[0]
        block_left = stat_left.shape[1]
        run = functools.partial(gather, n_shard=n_shard, n_tensor=n_tensor)

        moment_new = 0.9 * moment + 0.1 * gradient.astype(F32)
        third = rows_right // 3
        thirds = [part(basis_right, k, third, 0).astype(BF16) for k in range(3)]
        panel, left_blocks, right_0 = run(
            0, [gradient, lanes(basis_left.astype(BF16)), thirds[0]], []
        )
        panel = stacked(panel)
        first = s * rows_right
        owner = first // block_hidden
        strip = lax.dynamic_slice_in_dim(panel, first - owner * block_hidden, rows_right, 1)
        right_1, strip = run(
            1, [thirds[1]], [], casts=[strip], cast_ratio=(rows_right, block_hidden)
        )
        stat_right_new = 0.95 * stat_right + 0.05 * dot(strip, panel, 0, 0)
        cross_left = scatter_sum(dot(gradient, panel, 1, 1), t, n_tensor)
        stat_left_new = 0.95 * stat_left + 0.05 * cross_left
        right_2, stat_left_columns, stat_right_rows = run(
            2, [thirds[2], lanes(stat_left_new.astype(BF16))], [stat_right_new.astype(BF16)]
        )
        right_columns = stacked(jnp.concatenate([right_0, right_1, right_2], axis=1))

        power = dot(side_by_side(stat_right_rows), right_columns, 1, 0)
        power_half = power.astype(BF16)
        square = jnp.full((8, 128), jnp.sum(power * power), F32)
        power_panel, squares, left, grad_rows, moment_rows = run(
            3,
            [power_half, square],
            [lanes(left_blocks.reshape(-1, block_left)), gradient, moment_new.astype(BF16)],
        )
        left = side_by_side(left.reshape(n_tensor, n_shard * rows_left, block_left))
        rotated = jnp.concatenate([side_by_side(grad_rows), side_by_side(moment_rows)])
        rotated = dot(rotated, right_columns, 1, 0).astype(BF16)
        grad_right, moment_right = rotated[:rows_left], rotated[rows_left:]
        power_panel = stacked(power_panel)

        square = whole_sum(jnp.sum(squares[:, 0, 0]), n_tensor)
        scale = 1.0 / jnp.sqrt(square + 1e-06)
        mine = gram_half(power_half, power_panel, core, n_tensor)
        grad_right, moment_right, there = run(4, [grad_right, moment_right], [], [mine.astype(BF16)])
        mine = (((mine + there.astype(F32)) * scale) * scale).astype(BF16)
        halves = mine, swap(mine, 1, n_tensor)
        iterate = scale * (1.5 * power - 0.5 * apply_gram(halves, power_panel, core))

        basis_strip = part(left, s, rows_left, 1)
        grad_turned = dot(basis_strip, stacked(grad_right), 0, 0)
        moment_turned = dot(basis_strip, stacked(moment_right), 0, 0)
        second_new = 0.95 * second_moment + 0.05 * grad_turned * grad_turned
        scaled = (moment_turned / (jnp.sqrt(second_new) + 1e-08)).astype(BF16)
        terms = dot(scaled, right_columns, 1, 1).reshape(rows_left, n_tensor // 2, 2, block_hidden)
        terms = pick(terms, core, 2) + swap(pick(terms, 1 - core, 2), 1, n_tensor)
        back = pick(terms, t // 2, 1)

        def left_basis(stat_left_all):
            stat_all = side_by_side(stat_left_all.reshape(n_tensor, n_shard * rows_left, block_left))
            power_left = dot(stat_all, left, 1, 0)
            iterate_left = power_left / jnp.sqrt(jnp.sum(power_left * power_left) + 1e-06)
            for step in range(NS_ITERS):
                left_half = iterate_left.astype(BF16)
                if step < NS_ITERS - 1:
                    gram = dot(left_half, left_half, 1, 1).astype(BF16)
                    iterate_left = 1.5 * iterate_left - 0.5 * dot(gram, left_half, 1, 0)
                else:
                    gram = dot(part(left_half, s, rows_left, 0), left_half, 1, 1).astype(BF16)
                    own = part(part(iterate_left, s, rows_left, 0), t, block_left, 1)
                    iterate_left = 1.5 * own - 0.5 * dot(gram, part(left_half, t, block_left, 1), 1, 0)
            return iterate_left

        def gram_whole(mine, there):
            mine = (mine + there.astype(F32)).astype(BF16)
            return mine, swap(mine, 1, n_tensor)

        update = None
        for step in range(NS_ITERS - 1):
            iterate_half = iterate.astype(BF16)
            upper, lower = jnp.split(iterate_half, 2)
            if step == 0:
                upper, back_there = run(5, [upper], [], [pick(terms, 1 - t // 2, 1)])
                back_half = (back + back_there).astype(BF16)
            else:
                (upper,) = run(5 + 2 * step, [upper], [])
            upper = stacked(upper)
            mine_upper = gram_half(iterate_half, upper, core, n_tensor)
            if step == 0:
                lower, back_panel, stat_left_all, there_upper = run(
                    6, [lower, back_half], [lanes(stat_left_columns.reshape(-1, 128))], [mine_upper.astype(BF16)]
                )
                update = dot(part(left, s, rows_left, 0), stacked(back_panel), 1, 0)
            else:
                lower, there_upper = run(6 + 2 * step, [lower], [], [mine_upper.astype(BF16)])
            lower = stacked(lower)
            mine_lower = gram_half(iterate_half, lower, core, n_tensor)
            if step == NS_ITERS - 2:
                mine_lower, stat_left_all = lax.optimization_barrier((mine_lower, stat_left_all))
            there_lower = swap(mine_lower.astype(BF16), n_tensor // 2, n_tensor)
            halves = gram_whole(mine_upper, there_upper)
            change = apply_gram(halves, upper, core)
            if step == NS_ITERS - 2:
                there_lower, iterate_left, update, change = lax.optimization_barrier(
                    (there_lower, left_basis(stat_left_all), update, change)
                )
            change = change + apply_gram(gram_whole(mine_lower, there_lower), lower, core)
            iterate = 1.5 * iterate - 0.5 * change

        return (
            update,
            moment_new,
            second_new,
            stat_left_new,
            stat_right_new,
            iterate_left,
            iterate,
        )

    return per_device


def solution(mesh):
    spec = P("shard", "tensor")
    return jax.shard_map(
        make(mesh.shape["shard"], mesh.shape["tensor"]),
        mesh=mesh,
        in_specs=(spec,) * 7,
        out_specs=(spec,) * 7,
        check_vma=False,
    )
```
